128 devices in a mesh: gx: 4 (over z), gy: 4 (over y), gz: 8 (over x, core).
Axes of the slice: x: 4, y: 4, z: 4, core: 2. Of those that a mesh axis runs over, the one named last changes fastest.
Arguments:
- resident_basis: bfloat16 [5, 256, 16, 32, 2048], P(None, None, 'gx', 'gy', 'gz'), may hold values from -6 to 6
- block_basis: bfloat16 [2, 5, 32, 16, 32, 2048], P(None, None, None, 'gx', 'gy', 'gz'), may hold values from -6 to 6
- jacobian: bfloat16 [7, 5, 5, 16, 32, 2048], P(None, None, None, 'gx', 'gy', 'gz'), may hold values from -1 to 1
- volumes: float32 [16, 32, 2048], P('gx', 'gy', 'gz'), may hold values from 0.5 to 2
- cell_codes: int32 [16, 32, 2048], P('gx', 'gy', 'gz'), may hold values from 0 to 2
- phase_index: int32 [1], replicated, may hold values from 0 to 23
Outputs:
- reduced_jacobian: float32 [256, 64], replicated
- reduced_mass: float32 [256, 64], replicated
The draws below stay inside these ranges and needn't reach their ends.
All inputs are finite; a program needn't handle non-finite values.
Results may differ from the reference program's by a relative error of at most 0.0031.
Values may be sent and summed in bfloat16 or wider, within the bound.
A program may use at most 320 MiB of HBM per device.

```python
import math
import jax
import jax.numpy as jnp

FIELDS = 5
STENCIL = 7
RES = 256
BCOL = 32
NBLK = 2
BLADES = 24
NX = 16
NY = 32
NZ = 2048


def with_ends(drawn, own_key, smallest, top_value):
    spot = [jax.random.randint(jax.random.fold_in(own_key, axis), (), 0, length) for axis, length in enumerate(drawn.shape)]
    widest = drawn.shape.index(max(drawn.shape))
    next_to = spot[:widest] + [(spot[widest] + 1) % drawn.shape[widest]] + spot[widest + 1:]
    return drawn.at[tuple(spot)].set(smallest).at[tuple(next_to)].set(top_value)


def steps_of(own_key, dims, shards, least, high):
    factor_of = 1.0
    for dim, shards_of in shards:
        heights = jax.random.uniform(jax.random.fold_in(jax.random.fold_in(own_key, 6), dim), (shards_of,), jnp.float32, least / len(shards), high / len(shards))
        factor_of = factor_of * jnp.repeat(jnp.exp(heights), dims[dim] // shards_of).reshape((-1,) + (1,) * (len(dims) - 1 - dim))
    return factor_of


def normal_values(stream_key, dims, deviation, most, shards=(), dtype=jnp.bfloat16):
    values = deviation * jax.random.normal(stream_key, dims, jnp.float32)
    if shards:
        values = values * steps_of(stream_key, dims, shards, -0.22, 0.18)
    return jnp.clip(values, -most, most).astype(dtype)


def setup_inputs(seed: int = 0) -> dict:
    keys = jax.random.split(jax.random.key(seed), 7)
    return {
        "resident_basis": normal_values(keys[0], (FIELDS, RES, NX, NY, NZ), 1.0, 6.0, ((2, 4), (3, 4), (4, 8))),
        "block_basis": normal_values(keys[1], (NBLK, FIELDS, BCOL, NX, NY, NZ), 1.0, 6.0, ((3, 4), (4, 4), (5, 8))),
        "jacobian": normal_values(keys[2], (STENCIL, FIELDS, FIELDS, NX, NY, NZ), 35 ** -0.5, 1.0, ((3, 4), (4, 4), (5, 8))),
        "volumes": jnp.clip(jnp.exp(math.log(2.0) - 1.3862944 * jax.random.uniform(keys[3], (NX, NY, NZ), jnp.float32) ** steps_of(keys[3], (NX, NY, NZ), ((0, 4), (1, 4), (2, 8)), -0.2, 0.2)), 0.5, 2.0),
        "cell_codes": with_ends(jax.random.randint(keys[4], (NX, NY, NZ), 0, 3), jax.random.fold_in(keys[4], 1), 0, 2).astype(jnp.int32),
        "phase_index": jax.random.randint(keys[5], (1,), 0, BLADES).astype(jnp.int32),
    }


def extend_pair(real_part, imag_part, cosine, sine):
    re_vals = real_part.astype(jnp.float32)
    im_vals = imag_part.astype(jnp.float32)
    re_last = re_vals[:, :, :, -1:]
    im_last = im_vals[:, :, :, -1:]
    re_first = re_vals[:, :, :, :1]
    im_first = im_vals[:, :, :, :1]
    before_re = cosine * re_last + sine * im_last
    before_im = cosine * im_last - sine * re_last
    after_re = cosine * re_first - sine * im_first
    after_im = sine * re_first + cosine * im_first
    widths = ((0, 0), (0, 0), (1, 1), (0, 0), (1, 1))
    ext_re = jnp.pad(jnp.concatenate([before_re, re_vals, after_re], axis=3), widths)
    ext_im = jnp.pad(jnp.concatenate([before_im, im_vals, after_im], axis=3), widths)
    return [ext_re, ext_im]

def apply_block(block, extended, jacobian, penalty):
    sx, sy, sz = block.shape[-3:]
    near = [block.astype(jnp.float32), extended[:, :, 0:sx, 1:sy + 1, 1:sz + 1], extended[:, :, 2:sx + 2, 1:sy + 1, 1:sz + 1], extended[:, :, 1:sx + 1, 0:sy, 1:sz + 1], extended[:, :, 1:sx + 1, 2:sy + 2, 1:sz + 1], extended[:, :, 1:sx + 1, 1:sy + 1, 0:sz], extended[:, :, 1:sx + 1, 1:sy + 1, 2:sz + 2]]
    total = -penalty * block.astype(jnp.float32)
    for spot in range(STENCIL):
        for field in range(FIELDS):
            total = total + jacobian[spot, :, field][:, None].astype(jnp.float32) * near[spot][field][None]
    return total

def project(resident_basis, weighted):
    result = jnp.zeros((RES, weighted.shape[1]), jnp.float32)
    for field in range(FIELDS):
        left = resident_basis[field].reshape(RES, -1)
        right = weighted[field].reshape(weighted.shape[1], -1)
        result = result + jnp.dot(left, right.T, preferred_element_type=jnp.float32)
    return result

def reference(resident_basis, block_basis, jacobian, volumes, cell_codes, phase_index):
    sigma = 2.0 * math.pi * phase_index[0].astype(jnp.float32) / BLADES
    cosine = jnp.cos(sigma)
    sine = jnp.sin(sigma)
    far_cells = (cell_codes == 2).astype(jnp.float32)
    wall_cells = (cell_codes == 1).astype(jnp.float32)
    field_one = (jnp.arange(FIELDS) == 1).astype(jnp.float32)
    penalty = (far_cells[None] + 2.0 * wall_cells[None] * field_one[:, None, None, None])[:, None]
    scale = 1.0 / math.sqrt(FIELDS * NX * NY * NZ)
    extended_all = extend_pair(block_basis[0], block_basis[1], cosine, sine)
    stiff_cols = []
    mass_cols = []
    for blk in range(NBLK):
        block = block_basis[blk]
        applied = apply_block(block, extended_all[blk], jacobian, penalty)
        weighted = (volumes * applied).astype(jnp.bfloat16)
        massed = (volumes * block.astype(jnp.float32)).astype(jnp.bfloat16)
        stiff_cols.append(project(resident_basis, weighted))
        mass_cols.append(project(resident_basis, massed))
    reduced_jacobian = jnp.concatenate(stiff_cols, axis=1) * scale
    reduced_mass = jnp.concatenate(mass_cols, axis=1) * scale
    return (reduced_jacobian, reduced_mass)
```

```python
import functools
import math

import jax
import jax.numpy as jnp
from jax import lax
from jax.experimental import pallas as pl
from jax.experimental.pallas import tpu as pltpu
from jax.sharding import PartitionSpec as P

BLADES = 24
MESH = pl.DeviceIdType.MESH
NT = (((1,), (1,)), ((), ()))
F32 = jnp.float32
BF16 = jnp.bfloat16


def kernel(
    scale,
    basis_hbm,
    block_hbm,
    jac_hbm,
    vol_hbm,
    codes_hbm,
    phase_ref,
    stiff_out,
    mass_out,
    block_nat,
    jac_nat,
    vol,
    codes,
    ext,
    jac,
    basis,
    face_nat,
    face,
    rim_out,
    rim_in,
    col_out,
    col_in,
    partial,
    columns,
    total,
    gather1,
    gather2,
    gather3,
    local_sem,
    basis_sem,
    xs_sem,
    xr_sem,
    ys_sem,
    yr_sem,
    zs_sem,
    zr_sem,
    s1_sem,
    r1_sem,
    s2_sem,
    r2_sem,
    s3_sem,
    r3_sem,
):
    nb, nf, nc, nx, ny, nz = block_nat.shape
    nbc = nb * nc
    ix, iy, iz = (lax.axis_index(a) for a in ("gx", "gy", "gz"))
    cx, cy, cz = (lax.axis_size(a) for a in ("gx", "gy", "gz"))
    plane = cx * cy
    me2 = ix * cy + iy

    def in_plane(index):
        return (index // cy, index % cy, iz)

    def in_line(index):
        return (ix, iy, index)

    block_copies = [
        pltpu.make_async_copy(block_hbm.at[b], block_nat.at[b], local_sem.at[b]) for b in range(nb)
    ]
    jac_copy = pltpu.make_async_copy(jac_hbm, jac_nat, local_sem.at[nb])
    vol_copy = pltpu.make_async_copy(vol_hbm, vol, local_sem.at[nb + 1])
    codes_copy = pltpu.make_async_copy(codes_hbm, codes, local_sem.at[nb + 2])
    for copy in block_copies + [jac_copy, vol_copy, codes_copy]:
        copy.start()

    def basis_copy(x, slot):
        return pltpu.make_async_copy(
            basis_hbm.at[:, :, x], basis.at[slot], basis_sem.at[slot]
        )

    basis_order = (1, 2, 0, 3)
    basis_copy(basis_order[0], 0).start()

    barrier = pltpu.get_barrier_semaphore()
    for d in range(1, cz):
        pl.semaphore_signal(
            barrier, inc=1, device_id=in_line((iz + d) % cz), device_id_type=MESH
        )
    for d in range(1, plane):
        pl.semaphore_signal(
            barrier, inc=1, device_id=in_plane((me2 + d) % plane), device_id_type=MESH
        )
    pl.semaphore_wait(barrier, cz - 1 + plane - 1)

    def face_copy(side, b):
        source, target = ((nx - 1, (ix + 1) % cx), (0, (ix + cx - 1) % cx))[side]
        return pltpu.make_async_remote_copy(
            src_ref=block_hbm.at[b, :, :, source],
            dst_ref=face_nat.at[side, b],
            send_sem=xs_sem.at[side, b],
            recv_sem=xr_sem.at[side, b],
            device_id=(target, iy, iz),
            device_id_type=MESH,
        )

    for b in range(nb):
        for side in range(2):
            face_copy(side, b).start()

    for copy in block_copies:
        copy.wait()

    def relay(x, carry):
        def one(i, carry):
            b, f = i // nf, i % nf
            rows = jnp.swapaxes(block_nat[b, f, :, x], 0, 1)
            at = pl.ds(pl.multiple_of(b * nc, nc), nc)
            ext[x, pl.ds(1, ny), f, at] = rows.astype(F32)
            rim_out[1, x, f, at] = rows[0]
            rim_out[0, x, f, at] = rows[ny - 1]
            return carry

        return lax.fori_loop(0, nb * nf, one, carry)

    def rim_copy(side):
        target = ((iy + 1) % cy, (iy + cy - 1) % cy)[side]
        return pltpu.make_async_remote_copy(
            src_ref=rim_out.at[side],
            dst_ref=rim_in.at[side],
            send_sem=ys_sem.at[side],
            recv_sem=yr_sem.at[side],
            device_id=(ix, target, iz),
            device_id_type=MESH,
        )

    lax.fori_loop(0, nx, relay, 0)
    for side in range(2):
        rim_copy(side).start()

    lane = lax.broadcasted_iota(jnp.int32, (nf, nbc, 128), 2)
    col_out[...] = jnp.zeros_like(col_out)

    def pack(j, carry):
        x, y = j // ny, j % ny
        here = lane == j
        for f in range(nf):
            last = pltpu.roll(ext[x, 1 + y, f, :, nz - 128 :], j + 1, 1)
            first = pltpu.roll(ext[x, 1 + y, f, :, :128], j, 1)
            col_out[0, f] = jnp.where(here[f], last, col_out[0, f])
            col_out[1, f] = jnp.where(here[f], first, col_out[1, f])
        return carry

    lax.fori_loop(0, nx * ny, pack, 0)

    def col_copy(side):
        target = ((iz + 1) % cz, (iz + cz - 1) % cz)[side]
        return pltpu.make_async_remote_copy(
            src_ref=col_out.at[side],
            dst_ref=col_in.at[side],
            send_sem=zs_sem.at[side],
            recv_sem=zr_sem.at[side],
            device_id=in_line(target),
            device_id_type=MESH,
        )

    for side in range(2):
        col_copy(side).start()

    for copy in (jac_copy, vol_copy, codes_copy):
        copy.wait()

    count = 7 * nf * nf

    def blocks(x, carry):
        volume = vol[x]
        code = codes[x]
        far = jnp.where(code == 2, 1.0, 0.0).astype(F32)
        wall = jnp.where(code == 1, 2.0, 0.0).astype(F32)
        for first in range(0, count + 1, 8):
            group = []
            for k in range(first, first + 8):
                s, f, g = k // (nf * nf), (k // nf) % nf, k % nf
                if k == count:
                    value = volume
                else:
                    value = jac_nat[s, g, f, x].astype(F32)
                    if s == 0 and g == f:
                        value = value - (far + wall if g == 1 else far)
                    value = value * volume
                group.append(value)
            jac[x, :, pl.ds(first, 8)] = jnp.swapaxes(jnp.stack(group), 0, 1)
        return carry

    lax.fori_loop(0, nx, blocks, 0)

    for side in range(2):
        col_copy(side).wait()
    col_in[0] = col_in[0] * jnp.where(iz > 0, 1.0, 0.0).astype(F32)
    col_in[1] = col_in[1] * jnp.where(iz < cz - 1, 1.0, 0.0).astype(F32)

    lane2 = lax.broadcasted_iota(jnp.int32, (nc, 128), 1)
    halves = nz // 128

    def stencil(x, y, b, sides):
        at = pl.ds(pl.multiple_of(b * nc, nc), nc)
        j = x * ny + y
        for half in range(halves):
            lanes = pl.ds(half * 128, 128)
            acc = [None] * nf

            def add(s, f, values):
                for g in range(nf):
                    term = jac[x, y, pl.ds((s * nf + f) * nf + g, 1), lanes] * values
                    acc[g] = term if acc[g] is None else acc[g] + term

            for f in range(nf):
                here = ext[x, 1 + y, f, at, lanes]
                add(0, f, here)
                for s, xn in sides:
                    add(s, f, ext[xn, 1 + y, f, at, lanes])
                add(3, f, ext[x, y, f, at, lanes])
                add(4, f, ext[x, 2 + y, f, at, lanes])
                if half == 0:
                    before = pltpu.roll(col_in[0, f, at], (128 - j) % 128, 1)
                else:
                    before = pltpu.roll(ext[x, 1 + y, f, at, pl.ds(half * 128 - 128, 128)], 1, 1)
                add(5, f, jnp.where(lane2 == 0, before, pltpu.roll(here, 1, 1)))
                if half == halves - 1:
                    after = pltpu.roll(col_in[1, f, at], 127 - j, 1)
                else:
                    after = pltpu.roll(ext[x, 1 + y, f, at, pl.ds(half * 128 + 128, 128)], 127, 1)
                add(6, f, jnp.where(lane2 == 127, after, pltpu.roll(here, 127, 1)))
                mass = (here * jac[x, y, pl.ds(count, 1), lanes]).astype(BF16)
                columns[x, f, y, pl.ds(pl.multiple_of(nbc + b * nc, nc), nc), lanes] = mass
            yield half, lanes, acc

    def inner_row(x, y, b):
        at = pl.ds(pl.multiple_of(b * nc, nc), nc)
        for _, lanes, acc in stencil(x, y, b, ((1, x - 1), (2, x + 1))):
            for g in range(nf):
                columns[x, g, y, at, lanes] = acc[g].astype(BF16)

    def outer_row(k, y, b):
        at = pl.ds(pl.multiple_of(b * nc, nc), nc)
        x = k * (nx - 1)
        for _, lanes, acc in stencil(x, y, b, ((2 - k, 1 + k * (nx - 3)),)):
            for g in range(nf):
                partial[k, y, g, at, lanes] = acc[g]

    def rows(low, count, stride):
        def inner(i, carry):
            inner_row(1 + i // (count * nb), low + stride * ((i // nb) % count), i % nb)
            return carry

        lax.fori_loop(0, (nx - 2) * count * nb, inner, 0)
        for k in range(2):

            def outer(i, carry, k=k):
                outer_row(k, low + stride * (i // nb), i % nb)
                return carry

            lax.fori_loop(0, count * nb, outer, 0)

    rows(1, ny - 2, 1)

    phase = jnp.full((8, 128), phase_ref[0], jnp.int32).astype(F32)
    sigma = 2.0 * math.pi * phase / BLADES
    cosine = jnp.cos(sigma)[:1, :1]
    sine = jnp.sin(sigma)[:1, :1]
    for side in range(2):
        rim_copy(side).wait()
        at_end = (iy == 0, iy == cy - 1)[side]
        turn_c = jnp.where(at_end, cosine, 1.0)
        turn_s = jnp.where(at_end, sine if side == 0 else -sine, 0.0)
        row = 0 if side == 0 else ny + 1

        def turn(i, carry, side=side, row=row, turn_c=turn_c, turn_s=turn_s):
            x, f = i // nf, i % nf
            re = rim_in[side, x, f, :nc].astype(F32)
            im = rim_in[side, x, f, nc:].astype(F32)
            ext[x, row, f, :nc] = turn_c * re + turn_s * im
            ext[x, row, f, nc:] = turn_c * im - turn_s * re
            return carry

        lax.fori_loop(0, nx * nf, turn, 0)

    rows(0, 2, ny - 1)

    total[...] = jnp.zeros_like(total)

    def project(x, slot):
        def one(g, carry):
            left = jnp.swapaxes(basis[slot, g], 0, 1)
            left = jnp.concatenate([left[y] for y in range(ny)], axis=1)
            right = jnp.concatenate([columns[x, g, y] for y in range(ny)], axis=1)
            total[...] += lax.dot_general(left, right, NT, preferred_element_type=F32)
            return carry

        lax.fori_loop(0, nf, one, 0)

    basis_copy(basis_order[1], 1).start()
    for i in range(2):
        basis_copy(basis_order[i], i).wait()
        project(basis_order[i], i)
        basis_copy(basis_order[i + 2], i).start()

    keep = (jnp.where(ix > 0, 1.0, 0.0).astype(F32), jnp.where(ix < cx - 1, 1.0, 0.0).astype(F32))
    for b in range(nb):
        for side in range(2):
            face_copy(side, b).wait()
            for f in range(nf):
                face[side, :, f] = jnp.swapaxes(face_nat[side, b, f], 0, 1).astype(F32) * keep[side]

            def finish(y, carry, side=side, b=b):
                x = side * (nx - 1)
                at = pl.ds(b * nc, nc)
                for half in range(halves):
                    lanes = pl.ds(half * 128, 128)
                    acc = [partial[side, y, g, at, lanes] for g in range(nf)]
                    for f in range(nf):
                        values = face[side, y, f, :, lanes]
                        for g in range(nf):
                            acc[g] = acc[g] + jac[x, y, pl.ds(((1 + side) * nf + f) * nf + g, 1), lanes] * values
                    for g in range(nf):
                        columns[x, g, y, at, lanes] = acc[g].astype(BF16)
                return carry

            lax.fori_loop(0, ny, finish, 0)
    for i in range(2):
        basis_copy(basis_order[i + 2], i).wait()
        project(basis_order[i + 2], i)

    chunk = total.shape[0] // cz

    def copy1(d):
        target = (iz + d) % cz
        return pltpu.make_async_remote_copy(
            src_ref=total.at[pl.ds(pl.multiple_of(target * chunk, chunk), chunk)],
            dst_ref=gather1.at[d],
            send_sem=s1_sem.at[d],
            recv_sem=r1_sem.at[d],
            device_id=in_line(target),
            device_id_type=MESH,
        )

    for d in range(1, cz):
        copy1(d).start()
    own = total[pl.ds(pl.multiple_of(iz * chunk, chunk), chunk)]
    for d in range(1, cz):
        copy1(d).wait()
        own = own + gather1[d]
    gather2[me2] = own

    def copy2(d):
        return pltpu.make_async_remote_copy(
            src_ref=gather2.at[me2],
            dst_ref=gather2.at[me2],
            send_sem=s2_sem.at[d],
            recv_sem=r2_sem.at[d],
            device_id=in_plane((me2 + d) % plane),
            device_id_type=MESH,
        )

    for d in range(1, plane):
        copy2(d).start()
    for d in range(1, plane):
        copy2(d).wait()
    own = gather2[0]
    for i in range(1, plane):
        own = own + gather2[i]
    gather3[iz] = own * scale

    def copy3(d):
        return pltpu.make_async_remote_copy(
            src_ref=gather3.at[iz],
            dst_ref=gather3.at[iz],
            send_sem=s3_sem.at[d],
            recv_sem=r3_sem.at[d],
            device_id=in_line((iz + d) % cz),
            device_id_type=MESH,
        )

    for d in range(1, cz):
        copy3(d).start()
    for d in range(1, cz):
        copy3(d).wait()
    for i in range(cz):
        stiff_out[pl.ds(i * chunk, chunk)] = gather3[i, :, :nbc]
        mass_out[pl.ds(i * chunk, chunk)] = gather3[i, :, nbc:]


def shards(resident_basis, block_basis, jacobian, volumes, cell_codes, phase_index):
    nf, nr, nx, ny, nz = resident_basis.shape
    nb, _, nc = block_basis.shape[:3]
    nbc = nb * nc
    cx, cy, cz = (lax.axis_size(a) for a in ("gx", "gy", "gz"))
    scale = 1.0 / math.sqrt(nf * nx * ny * nz * cx * cy * cz)
    dma = pltpu.SemaphoreType.DMA
    anywhere = pl.BlockSpec(memory_space=pl.ANY)
    vmem = pl.BlockSpec(memory_space=pltpu.VMEM)
    out = jax.ShapeDtypeStruct((nr, nbc), F32)
    return pl.pallas_call(
        functools.partial(kernel, scale),
        out_shape=(out, out),
        in_specs=[anywhere] * 5 + [pl.BlockSpec(memory_space=pltpu.SMEM)],
        out_specs=(vmem, vmem),
        scratch_shapes=[
            pltpu.VMEM(block_basis.shape, BF16),
            pltpu.VMEM(jacobian.shape, BF16),
            pltpu.VMEM(volumes.shape, F32),
            pltpu.VMEM(cell_codes.shape, jnp.int32),
            pltpu.VMEM((nx, ny + 2, nf, nbc, nz), F32),
            pltpu.VMEM((nx, ny, 7 * nf * nf + 1, nz), F32),
            pltpu.VMEM((2, nf, nr, ny, nz), BF16),
            pltpu.VMEM((2, nb, nf, nc, ny, nz), BF16),
            pltpu.VMEM((2, ny, nf, nc, nz), F32),
            pltpu.VMEM((2, nx, nf, nbc, nz), BF16),
            pltpu.VMEM((2, nx, nf, nbc, nz), BF16),
            pltpu.VMEM((2, nf, nbc, 128), F32),
            pltpu.VMEM((2, nf, nbc, 128), F32),
            pltpu.VMEM((2, ny, nf, nbc, nz), F32),
            pltpu.VMEM((nx, nf, ny, 2 * nbc, nz), BF16),
            pltpu.VMEM((nr, 2 * nbc), F32),
            pltpu.VMEM((cz, nr // cz, 2 * nbc), F32),
            pltpu.VMEM((cx * cy, nr // cz, 2 * nbc), F32),
            pltpu.VMEM((cz, nr // cz, 2 * nbc), F32),
            dma((nb + 3,)),
            dma((2,)),
            dma((2, nb)),
            dma((2, nb)),
            dma((2,)),
            dma((2,)),
            dma((2,)),
            dma((2,)),
            dma((cz,)),
            dma((cz,)),
            dma((cx * cy,)),
            dma((cx * cy,)),
            dma((cz,)),
            dma((cz,)),
        ],
        compiler_params=pltpu.CompilerParams(
            collective_id=0, has_side_effects=True, vmem_limit_bytes=63 * 2**20
        ),
        name="galerkin",
    )(resident_basis, block_basis, jacobian, volumes, cell_codes, phase_index)


def solution(mesh):
    return jax.shard_map(
        shards,
        mesh=mesh,
        in_specs=(
            P(None, None, "gx", "gy", "gz"),
            P(None, None, None, "gx", "gy", "gz"),
            P(None, None, None, "gx", "gy", "gz"),
            P("gx", "gy", "gz"),
            P("gx", "gy", "gz"),
            P(),
        ),
        out_specs=(P(), P()),
        check_vma=False,
    )
```

```python
import math

import jax
import jax.numpy as jnp
from jax import lax
from jax.experimental import pallas as pl
from jax.experimental.pallas import tpu as pltpu
from jax.sharding import PartitionSpec as P

BLADES = 24
MESH = pl.DeviceIdType.MESH
NT = (((1,), (1,)), ((), ()))
F32 = jnp.float32
BF16 = jnp.bfloat16


def kernel(
    basis_hbm,
    block_hbm,
    jac_hbm,
    vol_hbm,
    codes_hbm,
    phase_ref,
    sums_out,
    block_nat,
    jac_nat,
    vol,
    codes,
    ext,
    jac,
    basis_nat,
    swapped_a,
    swapped_b,
    face_nat,
    face,
    rim_out,
    rim_in,
    col_out,
    col_in,
    col,
    partial,
    done_a,
    done_b,
    total,
    sums,
    gather1,
    gather2,
    gather3,
    local_sem,
    basis_sem,
    xs_sem,
    xr_sem,
    ys_sem,
    yr_sem,
    zs_sem,
    zr_sem,
    s1_sem,
    r1_sem,
    s2_sem,
    r2_sem,
    s3_sem,
    r3_sem,
):
    nb, nf, nc, nx, ny, nz = block_nat.shape
    nbc = nb * nc
    ix, iy, iz = (lax.axis_index(a) for a in ("gx", "gy", "gz"))
    cx, cy, cz = (lax.axis_size(a) for a in ("gx", "gy", "gz"))
    plane = cx * cy
    me2 = ix * cy + iy

    def in_plane(index):
        return (index // cy, index % cy, iz)

    def in_line(index):
        return (ix, iy, index)

    block_copies = [
        pltpu.make_async_copy(block_hbm.at[b], block_nat.at[b], local_sem.at[b]) for b in range(nb)
    ]
    jac_copy = pltpu.make_async_copy(jac_hbm, jac_nat, local_sem.at[nb])
    vol_copy = pltpu.make_async_copy(vol_hbm, vol, local_sem.at[nb + 1])
    codes_copy = pltpu.make_async_copy(codes_hbm, codes, local_sem.at[nb + 2])
    for copy in block_copies + [jac_copy, vol_copy, codes_copy]:
        copy.start()

    order = (1, 2, 0, 3)
    piece = basis_nat.shape[1] // ny

    def basis_copy(x, i):
        at = pl.ds(pl.multiple_of(i * piece, piece), piece)
        return pltpu.make_async_copy(basis_hbm.at[:, at, x], basis_nat.at[:, at], basis_sem.at[i])

    barrier = pltpu.get_barrier_semaphore()
    for d in range(1, cz):
        pl.semaphore_signal(
            barrier, inc=1, device_id=in_line((iz + d) % cz), device_id_type=MESH
        )
    for d in range(1, plane):
        pl.semaphore_signal(
            barrier, inc=1, device_id=in_plane((me2 + d) % plane), device_id_type=MESH
        )

    def face_copy(side, b):
        source, target = ((nx - 1, (ix + 1) % cx), (0, (ix + cx - 1) % cx))[side]
        return pltpu.make_async_remote_copy(
            src_ref=block_hbm.at[b, :, :, source],
            dst_ref=face_nat.at[side, b],
            send_sem=xs_sem.at[side, b],
            recv_sem=xr_sem.at[side, b],
            device_id=(target, iy, iz),
            device_id_type=MESH,
        )

    lane = lax.broadcasted_iota(jnp.int32, (nc, 128), 1)

    def relay(i, carry):
        b, f = i // nf, i % nf
        at = pl.ds(pl.multiple_of(b * nc, nc), nc)
        last = jnp.zeros((nc, 128), F32)
        first = jnp.zeros((nc, 128), F32)
        for x in range(nx):
            rows = jnp.swapaxes(block_nat[b, f, :, x], 0, 1)
            wide = rows.astype(F32)
            ext[x, pl.ds(1, ny), f, at] = wide
            rim_out[1, x, f, at] = rows[0]
            rim_out[0, x, f, at] = rows[ny - 1]
            for y in range(ny):
                j = x * ny + y
                last = jnp.where(lane == j, pltpu.roll(wide[y, :, nz - 128 :], (j + 1) % 128, 1), last)
                first = jnp.where(lane == j, pltpu.roll(wide[y, :, :128], j, 1), first)
        col_out[0, f, at] = last.astype(BF16)
        col_out[1, f, at] = first.astype(BF16)
        return carry

    def first_basis(i, carry):
        basis_copy(order[0], i).start()
        return carry

    for b in range(nb):
        if b == nb - 1:
            pl.semaphore_wait(barrier, cz - 1 + plane - 1)
            for part in range(nb):
                for side in range(2):
                    face_copy(side, part).start()
        block_copies[b].wait()
        if b == nb - 1:
            lax.fori_loop(0, ny, first_basis, 0)
        lax.fori_loop(b * nf, (b + 1) * nf, relay, 0)

    def col_copy(side):
        target = ((iz + 1) % cz, (iz + cz - 1) % cz)[side]
        return pltpu.make_async_remote_copy(
            src_ref=col_out.at[side],
            dst_ref=col_in.at[side],
            send_sem=zs_sem.at[side],
            recv_sem=zr_sem.at[side],
            device_id=in_line(target),
            device_id_type=MESH,
        )

    def rim_copy(side, x):
        target = ((iy + 1) % cy, (iy + cy - 1) % cy)[side]
        return pltpu.make_async_remote_copy(
            src_ref=rim_out.at[side, x],
            dst_ref=rim_in.at[side, x],
            send_sem=ys_sem.at[side, x],
            recv_sem=yr_sem.at[side, x],
            device_id=(ix, target, iz),
            device_id_type=MESH,
        )

    for side in range(2):
        col_copy(side).start()
    for x in order:
        for side in range(2):
            rim_copy(side, x).start()

    for copy in (jac_copy, vol_copy, codes_copy):
        copy.wait()
    count = 7 * nf * nf

    def blocks(x, carry):
        volume = vol[x]
        code = codes[x]
        far = jnp.where(code == 2, 1.0, 0.0).astype(F32)
        wall = jnp.where(code == 1, 2.0, 0.0).astype(F32)
        for start in range(0, count + 1, 8):
            group = []
            for k in range(start, start + 8):
                s, f, g = k // (nf * nf), (k // nf) % nf, k % nf
                if k == count:
                    value = volume
                else:
                    value = jac_nat[s, g, f, x].astype(F32)
                    if s == 0 and g == f:
                        value = value - (far + wall if g == 1 else far)
                    value = value * volume
                group.append(value)
            jac[x, :, pl.ds(start, 8)] = jnp.swapaxes(jnp.stack(group), 0, 1)
        return carry

    lax.fori_loop(0, nx, blocks, 0)

    phase = jnp.full((8, 128), phase_ref[0], jnp.int32).astype(F32)
    sigma = 2.0 * math.pi * phase / BLADES
    cosine = jnp.cos(sigma)[:1, :1]
    sine = jnp.sin(sigma)[:1, :1]
    turn_c = (jnp.where(iy == 0, cosine, 1.0), jnp.where(iy == cy - 1, cosine, 1.0))
    turn_s = (jnp.where(iy == 0, sine, 0.0), jnp.where(iy == cy - 1, -sine, 0.0))
    keep_z = (jnp.where(iz > 0, 1.0, 0.0).astype(F32), jnp.where(iz < cz - 1, 1.0, 0.0).astype(F32))
    keep_x = (jnp.where(ix > 0, 1.0, 0.0).astype(F32), jnp.where(ix < cx - 1, 1.0, 0.0).astype(F32))

    def swap(n, i):
        at = pl.ds(pl.multiple_of(i * piece, piece), piece)
        basis_copy(order[n], i).wait()
        for g in range(nf):
            (swapped_a, swapped_b)[n % 2][g, :, at] = jnp.swapaxes(basis_nat[g, at], 0, 1)
        if n < nx - 1:
            basis_copy(order[n + 1], i).start()

    for n in range(2):

        def early(i, carry, n=n):
            swap(n, i)
            return carry

        lax.fori_loop(0, ny, early, 0)

    for side in range(2):
        col_copy(side).wait()
        col[side] = col_in[side].astype(F32) * keep_z[side]

    halves = nz // 128

    def stencil(x, y, b, side, done, store):
        at = pl.ds(b * nc, nc)
        j = x * ny + y
        for half in range(halves):
            lanes = pl.ds(half * 128, 128)
            acc = [None] * nf

            def add(s, f, values):
                for g in range(nf):
                    term = jac[x, y, pl.ds((s * nf + f) * nf + g, 1), lanes] * values
                    acc[g] = term if acc[g] is None else acc[g] + term

            for f in range(nf):
                here = ext[x, 1 + y, f, at, lanes]
                add(0, f, here)
                for s, xn in ((1, x - 1), (2, x + 1)):
                    if 0 <= xn < nx:
                        add(s, f, ext[xn, 1 + y, f, at, lanes])
                    elif side == 1 or b == 0:
                        add(s, f, face[b if side else 0, y, f, :, lanes])
                add(3, f, ext[x, y, f, at, lanes])
                add(4, f, ext[x, 2 + y, f, at, lanes])
                if half == 0:
                    before = pltpu.roll(col[0, f, at], (128 - j) % 128, 1)
                else:
                    before = pltpu.roll(ext[x, 1 + y, f, at, pl.ds(half * 128 - 128, 128)], 1, 1)
                add(5, f, jnp.where(lane == 0, before, pltpu.roll(here, 1, 1)))
                if half == halves - 1:
                    after = pltpu.roll(col[1, f, at], 127 - j, 1)
                else:
                    after = pltpu.roll(ext[x, 1 + y, f, at, pl.ds(half * 128 + 128, 128)], 127, 1)
                add(6, f, jnp.where(lane == 127, after, pltpu.roll(here, 127, 1)))
                mass = (here * jac[x, y, pl.ds(count, 1), lanes]).astype(BF16)
                done[f, y, pl.ds(nbc + b * nc, nc), lanes] = mass
            for g in range(nf):
                store(b, g, lanes, acc[g])

    total[...] = jnp.zeros_like(total)
    for done in (done_a, done_b):
        for g in range(nf):
            done[g, ny] = jnp.zeros(done.shape[2:], BF16)

    def project(y, swapped, done, row):
        left = jnp.concatenate([swapped[g, y] for g in range(nf)], axis=1)
        right = jnp.concatenate([done[g, row] for g in range(nf)], axis=1)
        total[...] += lax.dot_general(left, right, NT, preferred_element_type=F32)

    def load_face(side, b, slot):
        face_copy(side, b).wait()

        def one(f, carry):
            rows = jnp.swapaxes(face_nat[side, b, f], 0, 1).astype(F32)
            face[slot, :, f] = rows * keep_x[side]
            return carry

        lax.fori_loop(0, nf, one, 0)

    def finish(y):
        for half in range(halves):
            lanes = pl.ds(half * 128, 128)
            acc = [partial[y, g, :, lanes] for g in range(nf)]
            for f in range(nf):
                values = face[2, y, f, :, lanes]
                for g in range(nf):
                    acc[g] = acc[g] + jac[0, y, pl.ds((nf + f) * nf + g, 1), lanes] * values
            for g in range(nf):
                done_a[g, y, pl.ds(nc, nc), lanes] = acc[g].astype(BF16)

    swaps = (swapped_a, swapped_b)
    dones = (done_a, done_b)
    for n, x in enumerate(order):
        done = dones[n % 2]
        side = 0 if x == 0 else 1 if x == nx - 1 else None
        if n == 2:
            load_face(0, 0, 0)
        if n == 3:

            def late(i, carry):
                swap(3, i)
                return carry

            lax.fori_loop(0, ny, late, 0)
            load_face(1, 0, 0)
            load_face(0, 1, 2)
            load_face(1, 1, 1)

        def row(i, carry, n=n, x=x, side=side, done=done):
            y = (i + 1) % ny

            @pl.when(i == ny - 2)
            def _():
                for t in range(2):
                    rim_copy(t, x).wait()

                    def turn(f, carry, t=t):
                        re = rim_in[t, x, f, :nc].astype(F32)
                        im = rim_in[t, x, f, nc:].astype(F32)
                        ext[x, t * (ny + 1), f, :nc] = turn_c[t] * re + turn_s[t] * im
                        ext[x, t * (ny + 1), f, nc:] = turn_c[t] * im - turn_s[t] * re
                        return carry

                    lax.fori_loop(0, nf, turn, 0)

            def store(b, g, lanes, value):
                if side == 0 and b == 1:
                    partial[y, g, :, lanes] = value
                else:
                    done[g, y, pl.ds(b * nc, nc), lanes] = value.astype(BF16)

            if n == 2:
                swap(n, i)
            if n == 1 or n == 2:
                project(i, swaps[1 - n % 2], dones[1 - n % 2], i)
            if n == 3:
                project((y + ny - 1) % ny, swapped_a, done_a, jnp.where(i == 0, ny, (y + ny - 1) % ny))
                project((y + ny - 1) % ny, swapped_b, done_b, jnp.where(i == 0, ny, (y + ny - 1) % ny))
                finish(y)
            for b in range(nb):
                stencil(x, y, b, side, done, store)
            return carry

        lax.fori_loop(0, ny, row, 0)

    project(0, swapped_a, done_a, 0)
    project(0, swapped_b, done_b, 0)

    sums[...] = total[...].T
    chunk = sums.shape[0] // cz

    def copy1(d):
        target = (iz + d) % cz
        return pltpu.make_async_remote_copy(
            src_ref=sums.at[pl.ds(pl.multiple_of(target * chunk, chunk), chunk)],
            dst_ref=gather1.at[d],
            send_sem=s1_sem.at[d],
            recv_sem=r1_sem.at[d],
            device_id=in_line(target),
            device_id_type=MESH,
        )

    for d in range(1, cz):
        copy1(d).start()
    own = sums[pl.ds(pl.multiple_of(iz * chunk, chunk), chunk)]
    for d in range(1, cz):
        copy1(d).wait()
        own = own + gather1[d]
    gather2[me2] = own

    def copy2(d):
        return pltpu.make_async_remote_copy(
            src_ref=gather2.at[me2],
            dst_ref=gather2.at[me2],
            send_sem=s2_sem.at[d],
            recv_sem=r2_sem.at[d],
            device_id=in_plane((me2 + d) % plane),
            device_id_type=MESH,
        )

    for d in range(1, plane):
        copy2(d).start()
    for d in range(1, plane):
        copy2(d).wait()
    own = gather2[0]
    for i in range(1, plane):
        own = own + gather2[i]
    gather3[iz] = own

    def copy3(d):
        return pltpu.make_async_remote_copy(
            src_ref=gather3.at[iz],
            dst_ref=gather3.at[iz],
            send_sem=s3_sem.at[d],
            recv_sem=r3_sem.at[d],
            device_id=in_line((iz + d) % cz),
            device_id_type=MESH,
        )

    for d in range(1, cz):
        copy3(d).start()
    for d in range(1, cz):
        copy3(d).wait()
    for i in range(cz):
        sums_out[pl.ds(i * chunk, chunk)] = gather3[i]


def shards(resident_basis, block_basis, jacobian, volumes, cell_codes, phase_index):
    nf, nr, nx, ny, nz = resident_basis.shape
    nb, _, nc = block_basis.shape[:3]
    nbc = nb * nc
    cx, cy, cz = (lax.axis_size(a) for a in ("gx", "gy", "gz"))
    scale = 1.0 / math.sqrt(nf * nx * ny * nz * cx * cy * cz)
    dma = pltpu.SemaphoreType.DMA
    anywhere = pl.BlockSpec(memory_space=pl.ANY)
    sums = pl.pallas_call(
        kernel,
        out_shape=jax.ShapeDtypeStruct((2 * nbc, nr), F32),
        in_specs=[anywhere] * 5 + [pl.BlockSpec(memory_space=pltpu.SMEM)],
        out_specs=pl.BlockSpec(memory_space=pltpu.VMEM),
        scratch_shapes=[
            pltpu.VMEM(block_basis.shape, BF16),
            pltpu.VMEM(jacobian.shape, BF16),
            pltpu.VMEM(volumes.shape, F32),
            pltpu.VMEM(cell_codes.shape, jnp.int32),
            pltpu.VMEM((nx, ny + 2, nf, nbc, nz), F32),
            pltpu.VMEM((nx, ny, 7 * nf * nf + 1, nz), F32),
            pltpu.VMEM((nf, nr, ny, nz), BF16),
            pltpu.VMEM((nf, ny, nr, nz), BF16),
            pltpu.VMEM((nf, ny, nr, nz), BF16),
            pltpu.VMEM((2, nb, nf, nc, ny, nz), BF16),
            pltpu.VMEM((3, ny, nf, nc, nz), F32),
            pltpu.VMEM((2, nx, nf, nbc, nz), BF16),
            pltpu.VMEM((2, nx, nf, nbc, nz), BF16),
            pltpu.VMEM((2, nf, nbc, 128), BF16),
            pltpu.VMEM((2, nf, nbc, 128), BF16),
            pltpu.VMEM((2, nf, nbc, 128), F32),
            pltpu.VMEM((ny, nf, nc, nz), F32),
            pltpu.VMEM((nf, ny + 1, 2 * nbc, nz), BF16),
            pltpu.VMEM((nf, ny + 1, 2 * nbc, nz), BF16),
            pltpu.VMEM((nr, 2 * nbc), F32),
            pltpu.VMEM((2 * nbc, nr), F32),
            pltpu.VMEM((cz, 2 * nbc // cz, nr), F32),
            pltpu.VMEM((cx * cy, 2 * nbc // cz, nr), F32),
            pltpu.VMEM((cz, 2 * nbc // cz, nr), F32),
            dma((nb + 3,)),
            dma((ny,)),
            dma((2, nb)),
            dma((2, nb)),
            dma((2, nx)),
            dma((2, nx)),
            dma((2,)),
            dma((2,)),
            dma((cz,)),
            dma((cz,)),
            dma((cx * cy,)),
            dma((cx * cy,)),
            dma((cz,)),
            dma((cz,)),
        ],
        compiler_params=pltpu.CompilerParams(
            collective_id=0, has_side_effects=True, vmem_limit_bytes=63 * 2**20
        ),
        name="galerkin",
    )(resident_basis, block_basis, jacobian, volumes, cell_codes, phase_index)
    return ((sums[:nbc] * scale).T, (sums[nbc:] * scale).T)


def solution(mesh):
    return jax.shard_map(
        shards,
        mesh=mesh,
        in_specs=(
            P(None, None, "gx", "gy", "gz"),
            P(None, None, None, "gx", "gy", "gz"),
            P(None, None, None, "gx", "gy", "gz"),
            P("gx", "gy", "gz"),
            P("gx", "gy", "gz"),
            P(),
        ),
        out_specs=(P(), P()),
        check_vma=False,
    )
```

```python
import math

import jax
import jax.numpy as jnp
from jax import lax
from jax.experimental import pallas as pl
from jax.experimental.pallas import tpu as pltpu
from jax.sharding import PartitionSpec as P

BLADES = 24
MESH = pl.DeviceIdType.MESH
NT = (((1,), (1,)), ((), ()))
F32 = jnp.float32
BF16 = jnp.bfloat16


def kernel(
    basis_hbm,
    block_hbm,
    jac_hbm,
    vol_hbm,
    codes_hbm,
    phase_ref,
    sums_out,
    block_nat,
    jac_nat,
    vol,
    codes,
    ext,
    jac,
    basis_nat,
    swapped_a,
    swapped_b,
    face_nat,
    face,
    rim_out,
    rim_in,
    col_out,
    col_in,
    col,
    done_a,
    done_b,
    done_c,
    total,
    sums,
    gather1,
    gather2,
    gather3,
    local_sem,
    basis_sem,
    xs_sem,
    xr_sem,
    ys_sem,
    yr_sem,
    zs_sem,
    zr_sem,
    s1_sem,
    r1_sem,
    s2_sem,
    r2_sem,
    s3_sem,
    r3_sem,
):
    nb, nf, nc, nx, ny, nz = block_nat.shape
    nbc = nb * nc
    ix, iy, iz = (lax.axis_index(a) for a in ("gx", "gy", "gz"))
    cx, cy, cz = (lax.axis_size(a) for a in ("gx", "gy", "gz"))
    plane = cx * cy
    me2 = ix * cy + iy

    def in_plane(index):
        return (index // cy, index % cy, iz)

    def in_line(index):
        return (ix, iy, index)

    block_copies = [
        pltpu.make_async_copy(block_hbm.at[b], block_nat.at[b], local_sem.at[b]) for b in range(nb)
    ]
    jac_copy = pltpu.make_async_copy(jac_hbm, jac_nat, local_sem.at[nb])
    vol_copy = pltpu.make_async_copy(vol_hbm, vol, local_sem.at[nb + 1])
    codes_copy = pltpu.make_async_copy(codes_hbm, codes, local_sem.at[nb + 2])
    for copy in block_copies + [jac_copy, vol_copy, codes_copy]:
        copy.start()

    order = (1, 2, 0, 3)
    piece = basis_nat.shape[1] // ny

    def basis_copy(x, i):
        at = pl.ds(pl.multiple_of(i * piece, piece), piece)
        return pltpu.make_async_copy(basis_hbm.at[:, at, x], basis_nat.at[:, at], basis_sem.at[i])

    barrier = pltpu.get_barrier_semaphore()
    for d in range(1, cz):
        pl.semaphore_signal(
            barrier, inc=1, device_id=in_line((iz + d) % cz), device_id_type=MESH
        )
    for d in range(1, plane):
        pl.semaphore_signal(
            barrier, inc=1, device_id=in_plane((me2 + d) % plane), device_id_type=MESH
        )

    def face_copy(side, b):
        source, target = ((nx - 1, (ix + 1) % cx), (0, (ix + cx - 1) % cx))[side]
        return pltpu.make_async_remote_copy(
            src_ref=block_hbm.at[b, :, :, source],
            dst_ref=face_nat.at[side, b],
            send_sem=xs_sem.at[side, b],
            recv_sem=xr_sem.at[side, b],
            device_id=(target, iy, iz),
            device_id_type=MESH,
        )

    lane = lax.broadcasted_iota(jnp.int32, (nc, 128), 1)

    def relay(i, carry):
        b, f = i // nf, i % nf
        at = pl.ds(pl.multiple_of(b * nc, nc), nc)
        last = jnp.zeros((nc, 128), F32)
        first = jnp.zeros((nc, 128), F32)
        for x in range(nx):
            rows = jnp.swapaxes(block_nat[b, f, :, x], 0, 1)
            wide = rows.astype(F32)
            ext[x, pl.ds(1, ny), f, at] = wide
            rim_out[1, x, f, at] = rows[0]
            rim_out[0, x, f, at] = rows[ny - 1]
            for y in range(ny):
                j = x * ny + y
                last = jnp.where(lane == j, pltpu.roll(wide[y, :, nz - 128 :], (j + 1) % 128, 1), last)
                first = jnp.where(lane == j, pltpu.roll(wide[y, :, :128], j, 1), first)
        col_out[0, f, at] = last.astype(BF16)
        col_out[1, f, at] = first.astype(BF16)
        return carry

    def first_basis(i, carry):
        basis_copy(order[0], i).start()
        return carry

    pl.semaphore_wait(barrier, cz - 1 + plane - 1)
    for part in range(nb):
        for side in range(2):
            face_copy(side, part).start()
    for b in range(nb):
        block_copies[b].wait()
        if b == nb - 1:
            lax.fori_loop(0, ny, first_basis, 0)
        lax.fori_loop(b * nf, (b + 1) * nf, relay, 0)

    def col_copy(side):
        target = ((iz + 1) % cz, (iz + cz - 1) % cz)[side]
        return pltpu.make_async_remote_copy(
            src_ref=col_out.at[side],
            dst_ref=col_in.at[side],
            send_sem=zs_sem.at[side],
            recv_sem=zr_sem.at[side],
            device_id=in_line(target),
            device_id_type=MESH,
        )

    def rim_copy(side, x):
        target = ((iy + 1) % cy, (iy + cy - 1) % cy)[side]
        return pltpu.make_async_remote_copy(
            src_ref=rim_out.at[side, x],
            dst_ref=rim_in.at[side, x],
            send_sem=ys_sem.at[side, x],
            recv_sem=yr_sem.at[side, x],
            device_id=(ix, target, iz),
            device_id_type=MESH,
        )

    for side in range(2):
        col_copy(side).start()
    for x in order:
        for side in range(2):
            rim_copy(side, x).start()

    for copy in (jac_copy, vol_copy, codes_copy):
        copy.wait()
    count = 7 * nf * nf

    def blocks(x, carry):
        volume = vol[x]
        code = codes[x]
        far = jnp.where(code == 2, 1.0, 0.0).astype(F32)
        wall = jnp.where(code == 1, 2.0, 0.0).astype(F32)
        for start in range(0, count + 1, 8):
            group = []
            for k in range(start, start + 8):
                s, f, g = k // (nf * nf), (k // nf) % nf, k % nf
                if k == count:
                    value = volume
                else:
                    value = jac_nat[s, g, f, x].astype(F32)
                    if s == 0 and g == f:
                        value = value - (far + wall if g == 1 else far)
                    value = value * volume
                group.append(value)
            jac[x, :, pl.ds(start, 8)] = jnp.swapaxes(jnp.stack(group), 0, 1)
        return carry

    lax.fori_loop(0, nx, blocks, 0)

    phase = jnp.full((8, 128), phase_ref[0], jnp.int32).astype(F32)
    sigma = 2.0 * math.pi * phase / BLADES
    cosine = jnp.cos(sigma)[:1, :1]
    sine = jnp.sin(sigma)[:1, :1]
    turn_c = (jnp.where(iy == 0, cosine, 1.0), jnp.where(iy == cy - 1, cosine, 1.0))
    turn_s = (jnp.where(iy == 0, sine, 0.0), jnp.where(iy == cy - 1, -sine, 0.0))
    keep_z = (jnp.where(iz > 0, 1.0, 0.0).astype(F32), jnp.where(iz < cz - 1, 1.0, 0.0).astype(F32))
    keep_x = (jnp.where(ix > 0, 1.0, 0.0).astype(F32), jnp.where(ix < cx - 1, 1.0, 0.0).astype(F32))

    def swap(n, i):
        at = pl.ds(pl.multiple_of(i * piece, piece), piece)
        basis_copy(order[n], i).wait()
        for g in range(nf):
            (swapped_a, swapped_b)[n % 2][g, :, at] = jnp.swapaxes(basis_nat[g, at], 0, 1)
        if n < nx - 1:
            basis_copy(order[n + 1], i).start()

    for n in range(2):

        def early(i, carry, n=n):
            swap(n, i)
            return carry

        lax.fori_loop(0, ny, early, 0)

    for side in range(2):
        col_copy(side).wait()
        col[side] = col_in[side].astype(F32) * keep_z[side]

    halves = nz // 128

    def stencil(x, y, b, side, done, store):
        at = pl.ds(b * nc, nc)
        j = x * ny + y
        for half in range(halves):
            lanes = pl.ds(half * 128, 128)
            acc = [None] * nf

            def add(s, f, values):
                for g in range(nf):
                    term = jac[x, y, pl.ds((s * nf + f) * nf + g, 1), lanes] * values
                    acc[g] = term if acc[g] is None else acc[g] + term

            for f in range(nf):
                here = ext[x, 1 + y, f, at, lanes]
                add(0, f, here)
                for s, xn in ((1, x - 1), (2, x + 1)):
                    if 0 <= xn < nx:
                        add(s, f, ext[xn, 1 + y, f, at, lanes])
                    else:
                        add(s, f, face[side, y, f, :, lanes])
                add(3, f, ext[x, y, f, at, lanes])
                add(4, f, ext[x, 2 + y, f, at, lanes])
                if half == 0:
                    before = pltpu.roll(col[0, f, at], (128 - j) % 128, 1)
                else:
                    before = pltpu.roll(ext[x, 1 + y, f, at, pl.ds(half * 128 - 128, 128)], 1, 1)
                add(5, f, jnp.where(lane == 0, before, pltpu.roll(here, 1, 1)))
                if half == halves - 1:
                    after = pltpu.roll(col[1, f, at], 127 - j, 1)
                else:
                    after = pltpu.roll(ext[x, 1 + y, f, at, pl.ds(half * 128 + 128, 128)], 127, 1)
                add(6, f, jnp.where(lane == 127, after, pltpu.roll(here, 127, 1)))
                mass = (here * jac[x, y, pl.ds(count, 1), lanes]).astype(BF16)
                done[f, y, pl.ds(nbc + b * nc, nc), lanes] = mass
            for g in range(nf):
                store(b, g, lanes, acc[g])

    total[...] = jnp.zeros_like(total)
    for done in (done_a, done_c):
        for g in range(nf):
            done[g, ny] = jnp.zeros(done.shape[2:], BF16)

    def project(y, swapped, done, row):
        left = jnp.concatenate([swapped[g, y] for g in range(nf)], axis=1)
        right = jnp.concatenate([done[g, row] for g in range(nf)], axis=1)
        total[...] += lax.dot_general(left, right, NT, preferred_element_type=F32)

    def load_face(side, b):
        face_copy(side, b).wait()

        def one(f, carry):
            rows = jnp.swapaxes(face_nat[side, b, f], 0, 1).astype(F32)
            face[side, :, f] = rows * keep_x[side]
            return carry

        lax.fori_loop(0, nf, one, 0)

    outer = ((0, 0, done_a), (nx - 1, 1, done_c))
    steps = (
        ((1, None, done_a, range(nb)),),
        ((2, None, done_b, range(nb)),),
        tuple(layer + ((0,),) for layer in outer),
        tuple(layer + ((1,),) for layer in outer),
    )
    for n, layers in enumerate(steps):
        if n == 2:
            for side in range(2):
                load_face(side, 0)
        if n == 3:

            def late(i, carry):
                swap(3, i)
                return carry

            lax.fori_loop(0, ny, late, 0)
            for side in range(2):
                load_face(side, 1)

        def row(i, carry, n=n, layers=layers):
            y = (i + 1) % ny

            if n < 3:

                @pl.when(i == ny - 2)
                def _():
                    for x, _side, _done, _parts in layers:
                        for t in range(2):
                            rim_copy(t, x).wait()

                            def turn(f, carry, x=x, t=t):
                                re = rim_in[t, x, f, :nc].astype(F32)
                                im = rim_in[t, x, f, nc:].astype(F32)
                                ext[x, t * (ny + 1), f, :nc] = turn_c[t] * re + turn_s[t] * im
                                ext[x, t * (ny + 1), f, nc:] = turn_c[t] * im - turn_s[t] * re
                                return carry

                            lax.fori_loop(0, nf, turn, 0)

            if n == 2:
                swap(n, i)
            if n == 1:
                project(i, swapped_a, done_a, i)
            if n == 2:
                project(i, swapped_b, done_b, i)
            if n == 3:
                before = (y + ny - 1) % ny
                project(before, swapped_a, done_a, jnp.where(i == 0, ny, before))
                project(before, swapped_b, done_c, jnp.where(i == 0, ny, before))
            for x, side, done, parts in layers:

                def store(b, g, lanes, value, done=done):
                    done[g, y, pl.ds(b * nc, nc), lanes] = value.astype(BF16)

                for b in parts:
                    stencil(x, y, b, side, done, store)
            return carry

        lax.fori_loop(0, ny, row, 0)

    project(0, swapped_a, done_a, 0)
    project(0, swapped_b, done_c, 0)

    sums[...] = total[...].T
    chunk = sums.shape[0] // cz

    def copy1(d):
        target = (iz + d) % cz
        return pltpu.make_async_remote_copy(
            src_ref=sums.at[pl.ds(pl.multiple_of(target * chunk, chunk), chunk)],
            dst_ref=gather1.at[d],
            send_sem=s1_sem.at[d],
            recv_sem=r1_sem.at[d],
            device_id=in_line(target),
            device_id_type=MESH,
        )

    far_line = sorted(range(1, cz), key=lambda d: -min(d, cz - d))
    for d in far_line:
        copy1(d).start()
    own = sums[pl.ds(pl.multiple_of(iz * chunk, chunk), chunk)]
    for d in range(1, cz):
        copy1(d).wait()
        own = own + gather1[d]
    gather2[me2] = own

    def copy2(d):
        return pltpu.make_async_remote_copy(
            src_ref=gather2.at[me2],
            dst_ref=gather2.at[me2],
            send_sem=s2_sem.at[d],
            recv_sem=r2_sem.at[d],
            device_id=((ix + d // cy) % cx, (iy + d % cy) % cy, iz),
            device_id_type=MESH,
        )

    far_plane = sorted(
        range(1, plane),
        key=lambda d: -(min(d // cy, cx - d // cy) + min(d % cy, cy - d % cy)),
    )
    for d in far_plane:
        copy2(d).start()
    for d in range(1, plane):
        copy2(d).wait()
    own = gather2[0]
    for i in range(1, plane):
        own = own + gather2[i]
    gather3[iz] = own

    def copy3(d):
        return pltpu.make_async_remote_copy(
            src_ref=gather3.at[iz],
            dst_ref=gather3.at[iz],
            send_sem=s3_sem.at[d],
            recv_sem=r3_sem.at[d],
            device_id=in_line((iz + d) % cz),
            device_id_type=MESH,
        )

    for d in far_line:
        copy3(d).start()
    for d in range(1, cz):
        copy3(d).wait()
    for i in range(cz):
        sums_out[pl.ds(i * chunk, chunk)] = gather3[i]


def shards(resident_basis, block_basis, jacobian, volumes, cell_codes, phase_index):
    nf, nr, nx, ny, nz = resident_basis.shape
    nb, _, nc = block_basis.shape[:3]
    nbc = nb * nc
    cx, cy, cz = (lax.axis_size(a) for a in ("gx", "gy", "gz"))
    scale = 1.0 / math.sqrt(nf * nx * ny * nz * cx * cy * cz)
    dma = pltpu.SemaphoreType.DMA
    anywhere = pl.BlockSpec(memory_space=pl.ANY)
    sums = pl.pallas_call(
        kernel,
        out_shape=jax.ShapeDtypeStruct((2 * nbc, nr), F32),
        in_specs=[anywhere] * 5 + [pl.BlockSpec(memory_space=pltpu.SMEM)],
        out_specs=pl.BlockSpec(memory_space=pltpu.VMEM),
        scratch_shapes=[
            pltpu.VMEM(block_basis.shape, BF16),
            pltpu.VMEM(jacobian.shape, BF16),
            pltpu.VMEM(volumes.shape, F32),
            pltpu.VMEM(cell_codes.shape, jnp.int32),
            pltpu.VMEM((nx, ny + 2, nf, nbc, nz), F32),
            pltpu.VMEM((nx, ny, 7 * nf * nf + 1, nz), F32),
            pltpu.VMEM((nf, nr, ny, nz), BF16),
            pltpu.VMEM((nf, ny, nr, nz), BF16),
            pltpu.VMEM((nf, ny, nr, nz), BF16),
            pltpu.VMEM((2, nb, nf, nc, ny, nz), BF16),
            pltpu.VMEM((2, ny, nf, nc, nz), F32),
            pltpu.VMEM((2, nx, nf, nbc, nz), BF16),
            pltpu.VMEM((2, nx, nf, nbc, nz), BF16),
            pltpu.VMEM((2, nf, nbc, 128), BF16),
            pltpu.VMEM((2, nf, nbc, 128), BF16),
            pltpu.VMEM((2, nf, nbc, 128), F32),
            pltpu.VMEM((nf, ny + 1, 2 * nbc, nz), BF16),
            pltpu.VMEM((nf, ny + 1, 2 * nbc, nz), BF16),
            pltpu.VMEM((nf, ny + 1, 2 * nbc, nz), BF16),
            pltpu.VMEM((nr, 2 * nbc), F32),
            pltpu.VMEM((2 * nbc, nr), F32),
            pltpu.VMEM((cz, 2 * nbc // cz, nr), F32),
            pltpu.VMEM((cx * cy, 2 * nbc // cz, nr), F32),
            pltpu.VMEM((cz, 2 * nbc // cz, nr), F32),
            dma((nb + 3,)),
            dma((ny,)),
            dma((2, nb)),
            dma((2, nb)),
            dma((2, nx)),
            dma((2, nx)),
            dma((2,)),
            dma((2,)),
            dma((cz,)),
            dma((cz,)),
            dma((cx * cy,)),
            dma((cx * cy,)),
            dma((cz,)),
            dma((cz,)),
        ],
        compiler_params=pltpu.CompilerParams(
            collective_id=0, has_side_effects=True, vmem_limit_bytes=63 * 2**20
        ),
        name="galerkin",
    )(resident_basis, block_basis, jacobian, volumes, cell_codes, phase_index)
    return ((sums[:nbc] * scale).T, (sums[nbc:] * scale).T)


def solution(mesh):
    return jax.shard_map(
        shards,
        mesh=mesh,
        in_specs=(
            P(None, None, "gx", "gy", "gz"),
            P(None, None, None, "gx", "gy", "gz"),
            P(None, None, None, "gx", "gy", "gz"),
            P("gx", "gy", "gz"),
            P("gx", "gy", "gz"),
            P(),
        ),
        out_specs=(P(), P()),
        check_vma=False,
    )
```
